1024 devices in a mesh: dp: 2 (over core), node: 64 (over y, x), chip: 8 (over z).
Axes of the slice: x: 8, y: 8, z: 8, core: 2. Of those that a mesh axis runs over, the one named last changes fastest.
Arguments:
- tokens: bfloat16 [8192, 2560], P(('dp', 'chip')), may hold values from -6 to 6
- slot_token: int32 [2, 8, 64, 16], P('dp', 'chip'), may hold values from 0 to 512, as said below
- grad_act: bfloat16 [256, 327680], P(None, ('dp', 'node', 'chip')), may hold values from -6 to 6
- w_up: bfloat16 [2560, 327680], P(None, ('dp', 'node', 'chip')), may hold values from -0.125 to 0.125
Outputs:
- grad_w_up: bfloat16 [2560, 327680], P(None, ('dp', 'node', 'chip'))
- grad_x: float32 [8192, 2560], P(('dp', 'chip'), 'node')
The draws below stay inside these ranges and needn't reach their ends.
Inputs may be any that keep to these rules, and one draw needn't show every extreme that they name: slot_token[s, c, e, m] indexes a token within the 512 rows of token shard (s, c); 512 marks an empty slot. Each block of 16 slots holds 1 to 16 distinct tokens first and then empty slots; some blocks of every expert are full.
All inputs are finite; a program needn't handle non-finite values.
Results may differ from the reference program's by a relative error of at most 0.015.
Values may be sent and summed in bfloat16 or wider, within the bound.
No kernel may reach another device: no remote copies, remote signals or barrier semaphores. Data moves between devices by JAX's collectives and lax.ppermute only.
A program may use at most 32 MiB of HBM per device.

```python
import jax
import jax.numpy as jnp
from jax import lax

D = 2560
HID = 5120
M = 16
TOK_GRP = 512
EXPERTS = 64
HID_DEV = 320
TOKENS = 8192
SLOTS = 256
N_DP = 2
N_CHIP = 8


def draw_slot_token(key, part):
    key = jax.random.fold_in(key, 5)
    perm_key, count_key = jax.random.split(key)
    blocks = N_DP * N_CHIP * EXPERTS
    chosen = jax.vmap(lambda each: jax.random.permutation(each, TOK_GRP))(jax.random.split(perm_key, blocks))[:, :M]
    count = jax.random.randint(count_key, (blocks,), 1, M + 1)
    label = jnp.arange(blocks, dtype=jnp.int32)
    count = jnp.where(label % 3 == 0, M, count)
    slot = jnp.arange(M, dtype=jnp.int32)
    filled = jnp.where(slot[None, :] < count[:, None], chosen, TOK_GRP)
    return filled.reshape(N_DP, N_CHIP, EXPERTS, M).astype(jnp.int32)


def levels(rng, shape, cuts, low, top_value):
    level = 1.0
    for axis_at, blocks in cuts:
        heights = jax.random.uniform(jax.random.fold_in(jax.random.fold_in(rng, 6), axis_at), (blocks,), jnp.float32, low / len(cuts), top_value / len(cuts))
        level = level * jnp.repeat(jnp.exp(heights), shape[axis_at] // blocks).reshape((-1,) + (1,) * (len(shape) - 1 - axis_at))
    return level


def scatter_about(rng, extent, deviation, reach, pieces=(), held_as=jnp.bfloat16):
    loudness = levels(rng, extent, pieces, -0.22, 0.18) if pieces else 1.0
    drawn = jax.random.normal(rng, extent, jnp.float32) * deviation * loudness
    return jnp.minimum(jnp.maximum(drawn, -reach), reach).astype(held_as)


def setup_inputs(seed: int = 0) -> dict:
    streams_of = jax.random.split(jax.random.key(seed), 5)
    return {
        "tokens": scatter_about(streams_of[0], (TOKENS, D), 1.0, 6.0, ((0, 16),)),
        "slot_token": draw_slot_token(jax.random.fold_in(streams_of[4], 71), 0),
        "grad_act": scatter_about(streams_of[2], (SLOTS, EXPERTS * HID), 1.0, 6.0, ((1, 1024),)),
        "w_up": scatter_about(streams_of[3], (D, EXPERTS * HID), D ** -0.5, 0.125, ((1, 1024),)),
    }


def gelu_slope(value):
    scale = 0.7978845608
    cubic = 0.044715
    inner = jnp.tanh(scale * (value + cubic * value * value * value))
    return 0.5 * (1.0 + inner) + 0.5 * value * (1.0 - inner * inner) * scale * (1.0 + 3.0 * cubic * value * value)


def reference(tokens, slot_token, grad_act, w_up):
    lists = jnp.transpose(slot_token, (1, 0, 2, 3))
    shard = (jnp.arange(N_DP, dtype=jnp.int32)[None, :] * N_CHIP + jnp.arange(N_CHIP, dtype=jnp.int32)[:, None]).astype(jnp.int32)
    groups = 2 * N_CHIP

    def one_expert(carry, expert):
        local = lax.dynamic_index_in_dim(lists, expert, 2, keepdims=False)
        valid = (local < TOK_GRP).reshape(-1, 1)
        index = (shard[:, :, None] * TOK_GRP + jnp.minimum(local, TOK_GRP - 1)).reshape(-1).astype(jnp.int32)
        rows_e = jnp.where(valid, tokens[index], jnp.zeros((), jnp.bfloat16)).astype(jnp.bfloat16)
        weight = lax.dynamic_slice_in_dim(w_up, expert * HID, HID, 1)
        grad = lax.dynamic_slice_in_dim(grad_act, expert * HID, HID, 1)
        pre_e = jnp.dot(rows_e, weight, preferred_element_type=jnp.float32)
        dh_e = (grad.astype(jnp.float32) * gelu_slope(pre_e)).astype(jnp.bfloat16)
        grad_w = jnp.dot(rows_e.T, dh_e, preferred_element_type=jnp.float32).astype(jnp.bfloat16)
        parts = jnp.einsum("sgh,dgh->gsd", dh_e.reshape(SLOTS, groups, HID_DEV).astype(jnp.float32),
                           weight.reshape(D, groups, HID_DEV).astype(jnp.float32))
        rounded = lax.optimization_barrier(parts.astype(jnp.bfloat16))
        summed = jnp.sum(rounded.astype(jnp.float32), axis=0)
        summed = jnp.where(valid, summed, jnp.zeros((), jnp.float32))
        return carry.at[index].add(summed), grad_w

    grad_x, grads = lax.scan(one_expert, jnp.zeros((TOKENS, D), jnp.float32), jnp.arange(EXPERTS, dtype=jnp.int32))
    grad_w_up = jnp.transpose(grads, (1, 0, 2)).reshape(D, EXPERTS * HID)
    return grad_w_up, grad_x
```

```python
import jax
import jax.numpy as jnp
from jax import lax
from jax.experimental import pallas as pl
from jax.experimental.pallas import tpu as pltpu
from jax.sharding import PartitionSpec as P

VMEM = pl.BlockSpec(memory_space=pltpu.VMEM)
SMEM = pl.BlockSpec(memory_space=pltpu.SMEM)
F32 = jnp.float32
BF16 = jnp.bfloat16
PARAMS = pltpu.CompilerParams(vmem_limit_bytes=48 * 1024 * 1024)

PIECES = (
    (0, 0), (0, 1),
    (-3, 0), (-3, 1),
    (3, 0), (3, 1),
    (-1, 0), (-1, 1),
    (1, 0), (1, 1),
    (2, 0), (2, 1), (4, 1),
    (-2, 0), (-2, 1), (4, 0),
)


def gelu_slope(value):
    scale = 0.7978845608
    cubic = 0.044715
    inner = jnp.tanh(scale * (value + cubic * value * value * value))
    return 0.5 * (1.0 + inner) + 0.5 * value * (1.0 - inner * inner) * scale * (
        1.0 + 3.0 * cubic * value * value
    )


def pick_kernel(place, slots, tokens, own, other):
    dp, node = place[0], place[1]
    experts = slots.shape[1] // 2
    lane = lax.broadcasted_iota(jnp.int32, slots.shape, 1)
    listed = slots[...]
    token = lax.broadcasted_iota(jnp.int32, (slots.shape[0], tokens.shape[0]), 1)
    for target, out in ((dp, own), (1 - dp, other)):
        expert = target * experts + node // 2
        column = jnp.sum(jnp.where(lane == expert, listed, 0), axis=1, keepdims=True)
        onehot = jnp.where(token == column, 1.0, 0.0).astype(BF16)
        out[...] = jnp.dot(onehot, tokens[...], preferred_element_type=F32).astype(BF16)


def expert_kernel(place, x0, p3, m3, a0, b0, a, b, wt, grad, near_m, near_p, far_m, far_p, keep, dh_out, rows):
    dp, chip = place[0], place[2]
    at = 0
    for ref in (x0, p3, m3, a0, b0, a, b):
        rows[at : at + ref.shape[0], :] = ref[...]
        at += ref.shape[0]
    slots = grad.shape[1]
    row = lax.broadcasted_iota(jnp.int32, (8, slots), 1)
    piece = row // 16
    column = jnp.zeros((8, slots), jnp.int32)
    for number, (offset, half) in enumerate(PIECES):
        first = (lax.rem(chip + offset + 8, 8) * 2 + lax.rem(dp + half, 2)) * 16
        column = jnp.where(piece == number, first, column)
    column = column + row - piece * 16
    given = lax.broadcasted_iota(jnp.int32, (slots, slots), 0)
    order = jnp.where(given == column[:1], 1.0, 0.0).astype(BF16)
    cotangent = jnp.dot(grad[...], order, preferred_element_type=F32)
    pre = lax.dot_general(wt[...], rows[...], (((1,), (1,)), ((), ())), preferred_element_type=F32)
    dh = (cotangent * gelu_slope(pre)).astype(BF16)
    dh_out[...] = dh
    width = wt.shape[1]
    step = 512
    for start in range(0, width, step):
        cols = slice(start, start + step)
        part = lax.dot_general(
            dh, wt[:, cols], (((0,), (0,)), ((), ())), preferred_element_type=F32
        ).astype(BF16)
        keep[:, cols] = part[0:96]
        near_m[:, cols] = part[96:128]
        near_p[:, cols] = part[128:160]
        far_m[0:32, cols] = part[160:192]
        far_p[32:48, cols] = part[192:208]
        far_p[0:32, cols] = part[208:240]
        far_m[32:48, cols] = part[240:256]


def weight_kernel(dh, x0, p3, m3, a0, b0, a, b, out, rows):
    at = 0
    for ref in (x0, p3, m3, a0, b0, a, b):
        rows[at : at + ref.shape[0], :] = ref[...]
        at += ref.shape[0]
    step = 512
    for start in range(0, out.shape[1], step):
        cols = slice(start, start + step)
        out[:, cols] = jnp.dot(dh[...], rows[:, cols], preferred_element_type=F32).astype(BF16)


def middle_kernel(keep, got_p, got_m, to_m, to_p):
    f = lambda value: value.astype(F32)
    to_m[0:16] = (f(keep[32:48]) + f(got_p[0:16]) + f(got_m[32:48])).astype(BF16)
    to_m[16:32] = (f(keep[48:64]) + f(got_p[16:32])).astype(BF16)
    to_p[0:16] = (f(keep[64:80]) + f(got_m[0:16])).astype(BF16)
    to_p[16:32] = (f(keep[80:96]) + f(got_m[16:32]) + f(got_p[32:48])).astype(BF16)


def last_kernel(keep, near_p, near_m, far_p, far_m, own, other):
    for start, out in ((0, own), (16, other)):
        at = slice(start, start + 16)
        out[...] = (
            keep[at].astype(F32)
            + near_p[at].astype(F32)
            + near_m[at].astype(F32)
            + far_p[at].astype(F32)
            + far_m[at].astype(F32)
        ).astype(BF16)


def pack_kernel(own, other, out):
    nodes = out.shape[0]
    wide = own.shape[1] // nodes
    gap = jnp.zeros((own.shape[0], 64 - wide), BF16)
    for node in range(nodes):
        cols = slice(node * wide, (node + 1) * wide)
        out[node] = jnp.concatenate([own[:, cols], gap, other[:, cols], gap], axis=1)


def spread_kernel(place, slots, arrived, out, onehot):
    dp = place[0]
    wide, tokens = out.shape
    depth = slots.shape[0]
    experts = slots.shape[1] // 2
    token = lax.broadcasted_iota(jnp.int32, (depth, tokens), 1)
    total = jnp.zeros((64, tokens), F32)
    for half in range(2):
        swap = lax.rem(dp + half, 2)
        listed = jnp.where(swap == 0, slots[:, :experts], slots[:, experts:])
        for expert in range(experts):
            column = listed[:, expert : expert + 1]
            onehot[expert * depth : (expert + 1) * depth, :] = jnp.where(
                token == column, 1.0, 0.0
            ).astype(BF16)
        for pair in range(2):
            got = arrived[:, pair, :, half * 64 : half * 64 + 64].reshape(experts * depth, 64)
            total += lax.dot_general(
                got, onehot[...], (((0,), (0,)), ((), ())), preferred_element_type=F32
            )
    out[...] = total[:wide]


def shape(rows, columns, dtype=BF16):
    return jax.ShapeDtypeStruct((rows, columns), dtype)


def body(tokens, slot_token, grad_act, w_up):
    tok_grp, width = tokens.shape
    hidden = w_up.shape[1]
    n_nodes = lax.axis_size("node")
    chips = lax.axis_size("chip")
    place = jnp.stack(
        [lax.axis_index("dp"), lax.axis_index("node"), lax.axis_index("chip")]
    ).astype(jnp.int32)
    slots = slot_token[0, 0].T
    depth = slots.shape[0]
    wt = w_up.T
    grad = grad_act.T

    def shift(value, by):
        return lax.ppermute(value, "chip", [(c, (c + by) % chips) for c in range(chips)])

    def swap(value):
        return lax.ppermute(value, "dp", [(0, 1), (1, 0)])

    block = 512
    own, other = pl.pallas_call(
        pick_kernel,
        grid=(width // block,),
        in_specs=[
            SMEM,
            pl.BlockSpec(slots.shape, lambda i: (0, 0)),
            pl.BlockSpec((tok_grp, block), lambda i: (0, i)),
        ],
        out_specs=[pl.BlockSpec((depth, block), lambda i: (0, i))] * 2,
        out_shape=[shape(depth, width)] * 2,
        compiler_params=PARAMS,
    )(place, slots, tokens)
    x0 = jnp.concatenate([own, swap(other)], 0)

    p3, m3 = shift(x0, 3), shift(x0, -3)
    a0, b0 = shift(x0, 1), shift(x0, -1)
    a = shift(jnp.concatenate([m3, p3[16:]], 0), 1)
    b = shift(jnp.concatenate([p3, m3[:16]], 0), -1)
    gathered = (x0, p3, m3, a0, b0, a, b)

    near_m, near_p, far_m, far_p, keep, dh = pl.pallas_call(
        expert_kernel,
        in_specs=[SMEM] + [VMEM] * 9,
        out_specs=[VMEM] * 6,
        out_shape=[
            shape(32, width),
            shape(32, width),
            shape(48, width),
            shape(48, width),
            shape(96, width),
            shape(hidden, 256),
        ],
        scratch_shapes=[pltpu.VMEM((256, width), BF16)],
        compiler_params=PARAMS,
    )(place, *gathered, wt, grad)

    got_p, got_m = shift(far_p, 1), shift(far_m, -1)
    direct_p, direct_m = shift(near_p, 1), shift(near_m, -1)
    grad_wt = pl.pallas_call(
        weight_kernel,
        in_specs=[VMEM] * 8,
        out_specs=VMEM,
        out_shape=shape(hidden, width),
        scratch_shapes=[pltpu.VMEM((256, width), BF16)],
        compiler_params=PARAMS,
        cost_estimate=pl.CostEstimate(flops=2 * 256 * hidden * width, bytes_accessed=5000000, transcendentals=0),
    )(dh, *gathered)
    to_m, to_p = pl.pallas_call(
        middle_kernel,
        in_specs=[VMEM] * 3,
        out_specs=[VMEM] * 2,
        out_shape=[shape(32, width)] * 2,
        compiler_params=PARAMS,
    )(keep, got_p, got_m)
    from_p, from_m = shift(to_p, 3), shift(to_m, -3)
    own_sum, other_sum = pl.pallas_call(
        last_kernel,
        in_specs=[VMEM] * 5,
        out_specs=[VMEM] * 2,
        out_shape=[shape(depth, width)] * 2,
        compiler_params=PARAMS,
    )(keep, direct_p, direct_m, from_p, from_m)
    packed = pl.pallas_call(
        pack_kernel,
        in_specs=[VMEM] * 2,
        out_specs=VMEM,
        out_shape=jax.ShapeDtypeStruct((n_nodes, depth, 128), BF16),
        compiler_params=PARAMS,
    )(own_sum, swap(other_sum))
    arrived = lax.all_to_all(packed, "node", 0, 0, tiled=True)
    grad_xt = pl.pallas_call(
        spread_kernel,
        in_specs=[SMEM, VMEM, VMEM],
        out_specs=VMEM,
        out_shape=shape(width // n_nodes, tok_grp, F32),
        scratch_shapes=[pltpu.VMEM((depth * n_nodes // 2, tok_grp), BF16)],
        compiler_params=PARAMS,
    )(place, slots, arrived.reshape(n_nodes // 2, 2, depth, 128))
    return (grad_wt.T, grad_xt.T)


def solution(mesh):
    placed = (
        P(("dp", "chip"), None),
        P("dp", "chip", None, None),
        P(None, ("dp", "node", "chip")),
        P(None, ("dp", "node", "chip")),
    )
    return jax.shard_map(
        body,
        mesh=mesh,
        in_specs=placed,
        out_specs=(P(None, ("dp", "node", "chip")), P(("dp", "chip"), "node")),
        check_vma=False,
    )
```

```python
import functools

import jax
import jax.numpy as jnp
from jax import lax
from jax.experimental import pallas as pl
from jax.experimental.pallas import tpu as pltpu
from jax.sharding import PartitionSpec as P

VMEM = pl.BlockSpec(memory_space=pltpu.VMEM)
HBM = pl.BlockSpec(memory_space=pltpu.HBM)
F32 = jnp.float32
BF16 = jnp.bfloat16
WAIT = pl.CostEstimate(flops=20_000_000_000, bytes_accessed=0, transcendentals=0)
PARAMS = pltpu.CompilerParams(vmem_limit_bytes=24 * 1024 * 1024)

HELD = (0, -2, 2, 4)
SENT = (-1, -3, 1, 3)


def gelu_slope(value):
    scale = 0.7978845608
    cubic = 0.044715
    inner = jnp.tanh(scale * (value + cubic * value * value * value))
    return 0.5 * (1.0 + inner) + 0.5 * value * (1.0 - inner * inner) * scale * (
        1.0 + 3.0 * cubic * value * value
    )


def pick_kernel(slots_from, tokens_from, own, other, slots, tokens, done):
    dp, node = lax.axis_index("dp"), lax.axis_index("node")
    depth = slots.shape[0]
    experts = slots.shape[1] // 2
    step = 512
    lists = pltpu.make_async_copy(slots_from, slots, done.at[0])
    lists.start()
    copies = []
    for number, start in enumerate(range(0, tokens.shape[1], step)):
        cols = pl.ds(start, step)
        copies.append(
            pltpu.make_async_copy(tokens_from.at[:, cols], tokens.at[:, cols], done.at[number + 1])
        )
        copies[-1].start()
    lists.wait()
    lane = lax.broadcasted_iota(jnp.int32, slots.shape, 1)
    listed = slots[...]
    token = lax.broadcasted_iota(jnp.int32, (2 * depth, tokens.shape[0]), 1)
    columns = [
        jnp.sum(jnp.where(lane == target * experts + node // 2, listed, 0), axis=1, keepdims=True)
        for target in (dp, 1 - dp)
    ]
    onehot = jnp.where(token == jnp.concatenate(columns, axis=0), 1.0, 0.0).astype(BF16)
    for number, start in enumerate(range(0, tokens.shape[1], step)):
        cols = slice(start, start + step)
        copies[number].wait()
        rows = jnp.dot(onehot, tokens[:, cols], preferred_element_type=F32).astype(BF16)
        own[:, cols] = rows[:depth]
        other[:, cols] = rows[depth:]


def prepare_kernel(slots, grad, held, sent, onehot):
    dp, chip = lax.axis_index("dp"), lax.axis_index("chip")
    total = grad.shape[1]
    for blocks, out in ((HELD, held), (SENT, sent)):
        count = 32 * len(blocks)
        row = lax.broadcasted_iota(jnp.int32, (8, count), 1)
        block = row // 32
        half = row // 16 - 2 * block
        column = row - 16 * (row // 16) + 16 * jnp.where(half == 0, dp, 1 - dp)
        for number, offset in enumerate(blocks):
            first = lax.rem(chip + offset + 8, 8) * 32
            column = jnp.where(block == number, column + first, column)
        given = lax.broadcasted_iota(jnp.int32, (total, count), 0)
        order = jnp.where(given == column[:1], 1.0, 0.0).astype(BF16)
        out[...] = jnp.dot(grad[...], order, preferred_element_type=F32).astype(BF16)
    depth = slots.shape[0]
    experts = slots.shape[1] // 2
    tokens = onehot.shape[2]
    token = lax.broadcasted_iota(jnp.int32, (depth, tokens), 1)
    for half in range(2):
        swap = lax.rem(dp + half, 2)
        listed = jnp.where(swap == 0, slots[:, :experts], slots[:, experts:])
        for expert in range(experts):
            column = listed[:, expert : expert + 1]
            onehot[half, expert * depth : (expert + 1) * depth, :] = jnp.where(
                token == column, 1.0, 0.0
            ).astype(BF16)


def fill(rows, *pieces):
    at = 0
    for ref in pieces:
        rows[at : at + ref.shape[0], :] = ref[...]
        at += ref.shape[0]


def expert_kernel(pieces, *refs):
    given, wt, grad = refs[:pieces], refs[pieces], refs[pieces + 1]
    parts, dh_out, rows = refs[pieces + 2 : -2], refs[-2], refs[-1]
    fill(rows, *given)
    pre = lax.dot_general(wt[...], rows[...], (((1,), (1,)), ((), ())), preferred_element_type=F32)
    dh = (grad[...].astype(F32) * gelu_slope(pre)).astype(BF16)
    dh_out[...] = dh
    step = 512
    for start in range(0, wt.shape[1], step):
        cols = slice(start, start + step)
        part = lax.dot_general(
            dh, wt[:, cols], (((0,), (0,)), ((), ())), preferred_element_type=F32
        ).astype(BF16)
        at = 0
        for out in parts:
            out[:, cols] = part[at : at + out.shape[0]]
            at += out.shape[0]


def join_kernel(x0, p2, m2, to_p, to_m):
    fill(to_p, x0, p2)
    fill(to_m, x0, m2)


def weight_kernel(dh_held, dh_sent, x0, p2, m2, p1, m1, far, out, rows, dh):
    fill(rows, x0, p2, m2, far, p1, m1)
    at = 0
    for ref in (dh_held, dh_sent):
        dh[:, at : at + ref.shape[1]] = ref[...]
        at += ref.shape[1]
    step = 512
    for start in range(0, out.shape[1], step):
        cols = slice(start, start + step)
        out[:, cols] = jnp.dot(dh[...], rows[:, cols], preferred_element_type=F32).astype(BF16)


def middle_kernel(keep, got_p, got_m, to_p, to_m):
    f = lambda value: value.astype(F32)
    to_m[...] = (f(keep[32:64]) + f(got_m[32:64])).astype(BF16)
    to_p[...] = (f(keep[64:96]) + f(got_p[32:64])).astype(BF16)


def across_kernel(keep, across, out):
    out[...] = keep[0:32].astype(F32) + across[...].astype(F32)


def last_kernel(near, got_p, got_m, from_p, from_m, own, other):
    for start, out in ((0, own), (16, other)):
        at = slice(start, start + 16)
        total = near[at]
        for ref in (got_p, got_m, from_p, from_m):
            total = total + ref[at].astype(F32)
        out[...] = total.astype(BF16)


def pack_kernel(own, other, out):
    nodes = out.shape[0]
    wide = own.shape[1] // nodes
    gap = jnp.zeros((own.shape[0], 64 - wide), BF16)
    for node in range(nodes):
        cols = slice(node * wide, (node + 1) * wide)
        out[node] = jnp.concatenate([own[:, cols], gap, other[:, cols], gap], axis=1)


def spread_kernel(onehot, arrived, out):
    wide, tokens = out.shape
    total = jnp.zeros((64, tokens), F32)
    for half in range(2):
        for pair in range(2):
            got = arrived[:, pair, :, half * 64 : half * 64 + 64].reshape(onehot.shape[1], 64)
            total += lax.dot_general(
                got, onehot[half], (((0,), (0,)), ((), ())), preferred_element_type=F32
            )
    out[...] = total[:wide]


def shape(rows, columns, dtype=BF16):
    return jax.ShapeDtypeStruct((rows, columns), dtype)


def body(tokens, slot_token, grad_act, w_up):
    tok_grp, width = tokens.shape
    hidden = w_up.shape[1]
    n_nodes = lax.axis_size("node")
    chips = lax.axis_size("chip")
    slots = slot_token[0, 0].T
    depth = slots.shape[0]
    wt = w_up.T
    grad = grad_act.T

    def shift(value, by):
        return lax.ppermute(value, "chip", [(c, (c + by) % chips) for c in range(chips)])

    def swap(value):
        return lax.ppermute(value, "dp", [(0, 1), (1, 0)])

    own, other = pl.pallas_call(
        pick_kernel,
        in_specs=[HBM] * 2,
        out_specs=[VMEM] * 2,
        out_shape=[shape(depth, width)] * 2,
        scratch_shapes=[
            pltpu.VMEM(slots.shape, jnp.int32),
            pltpu.VMEM(tokens.shape, BF16),
            pltpu.SemaphoreType.DMA((width // 512 + 1,)),
        ],
        compiler_params=pltpu.CompilerParams(vmem_limit_bytes=62 * 1024 * 1024),
    )(slots, tokens)
    x0 = jnp.concatenate([own, swap(other)], 0)

    def expert(rows, cotangent, sizes, cost=None):
        count = cotangent.shape[1]
        return pl.pallas_call(
            functools.partial(expert_kernel, len(rows)),
            in_specs=[VMEM] * (len(rows) + 2),
            out_specs=[VMEM] * (len(sizes) + 1),
            out_shape=[shape(size, width) for size in sizes] + [shape(hidden, count)],
            scratch_shapes=[pltpu.VMEM((count, width), BF16)],
            compiler_params=PARAMS,
            cost_estimate=cost
            or pl.CostEstimate(flops=4 * count * hidden * width, bytes_accessed=4000000, transcendentals=0),
        )(*rows, wt, cotangent)

    p2, m2 = shift(x0, 2), shift(x0, -2)
    far = shift(x0, 4)
    grad_held, grad_sent, onehot = pl.pallas_call(
        prepare_kernel,
        in_specs=[VMEM, VMEM],
        out_specs=[VMEM] * 3,
        out_shape=[
            shape(hidden, 128),
            shape(hidden, 128),
            jax.ShapeDtypeStruct((2, depth * n_nodes // 2, tok_grp), BF16),
        ],
        compiler_params=PARAMS,
    )(slots, grad)
    p2, grad_held, grad_sent, onehot = lax.optimization_barrier(
        (p2, grad_held, grad_sent, onehot)
    )
    to_p, to_m = pl.pallas_call(
        join_kernel,
        in_specs=[VMEM] * 3,
        out_specs=[VMEM] * 2,
        out_shape=[shape(64, width)] * 2,
        compiler_params=PARAMS,
        cost_estimate=WAIT,
    )(x0, p2, m2)
    p1, m1 = shift(to_p, 1), shift(to_m, -1)
    keep, to_far, dh_held = expert((x0, p2, m2, far), grad_held, (96, 32), WAIT)
    across = shift(to_far, 4)
    p1, keep, dh_held = lax.optimization_barrier((p1, keep, dh_held))
    to_m, to_p, dh_sent = expert((p1, m1), grad_sent, (64, 64))
    got_p, got_m = shift(to_p, 1), shift(to_m, -1)
    grad_wt = pl.pallas_call(
        weight_kernel,
        in_specs=[VMEM] * 8,
        out_specs=VMEM,
        out_shape=shape(hidden, width),
        scratch_shapes=[pltpu.VMEM((256, width), BF16), pltpu.VMEM((hidden, 256), BF16)],
        compiler_params=PARAMS,
        cost_estimate=pl.CostEstimate(flops=2 * 256 * hidden * width, bytes_accessed=5000000, transcendentals=0),
    )(dh_held, dh_sent, x0, p2, m2, p1, m1, far)
    near = pl.pallas_call(
        across_kernel,
        in_specs=[VMEM] * 2,
        out_specs=VMEM,
        out_shape=shape(32, width, F32),
        compiler_params=PARAMS,
        cost_estimate=WAIT,
    )(keep, across)
    got_p, got_m, near = lax.optimization_barrier((got_p, got_m, near))
    back_p, back_m = pl.pallas_call(
        middle_kernel,
        in_specs=[VMEM] * 3,
        out_specs=[VMEM] * 2,
        out_shape=[shape(32, width)] * 2,
        compiler_params=PARAMS,
        cost_estimate=WAIT,
    )(keep, got_p, got_m)
    from_p, from_m = shift(back_p, 2), shift(back_m, -2)
    from_p, from_m, grad_wt = lax.optimization_barrier((from_p, from_m, grad_wt))
    own_sum, other_sum = pl.pallas_call(
        last_kernel,
        in_specs=[VMEM] * 5,
        out_specs=[VMEM] * 2,
        out_shape=[shape(depth, width)] * 2,
        compiler_params=PARAMS,
    )(near, got_p, got_m, from_p, from_m)
    packed = pl.pallas_call(
        pack_kernel,
        in_specs=[VMEM] * 2,
        out_specs=VMEM,
        out_shape=jax.ShapeDtypeStruct((n_nodes, depth, 128), BF16),
        compiler_params=PARAMS,
    )(own_sum, swap(other_sum))
    arrived = lax.all_to_all(packed, "node", 0, 0, tiled=True)
    grad_xt = pl.pallas_call(
        spread_kernel,
        in_specs=[VMEM, VMEM],
        out_specs=VMEM,
        out_shape=shape(width // n_nodes, tok_grp, F32),
        compiler_params=PARAMS,
    )(onehot, arrived.reshape(n_nodes // 2, 2, depth, 128))
    return (grad_wt.T, grad_xt.T)


def solution(mesh):
    placed = (
        P(("dp", "chip"), None),
        P("dp", "chip", None, None),
        P(None, ("dp", "node", "chip")),
        P(None, ("dp", "node", "chip")),
    )
    return jax.shard_map(
        body,
        mesh=mesh,
        in_specs=placed,
        out_specs=(P(None, ("dp", "node", "chip")), P(("dp", "chip"), "node")),
        check_vma=False,
    )
```

```python
import functools

import jax
import jax.numpy as jnp
from jax import lax
from jax.experimental import pallas as pl
from jax.experimental.pallas import tpu as pltpu
from jax.sharding import PartitionSpec as P

VMEM = pl.BlockSpec(memory_space=pltpu.VMEM)
HBM = pl.BlockSpec(memory_space=pltpu.HBM)
F32 = jnp.float32
BF16 = jnp.bfloat16
WAIT = pl.CostEstimate(flops=20_000_000_000, bytes_accessed=0, transcendentals=0)
PARAMS = pltpu.CompilerParams(vmem_limit_bytes=24 * 1024 * 1024)

HELD = (0, -2, 2, 4)
SENT = (-1, -3, 1, 3)


def gelu_slope(value):
    scale = 0.7978845608
    cubic = 0.044715
    inner = jnp.tanh(scale * (value + cubic * value * value * value))
    return 0.5 * (1.0 + inner) + 0.5 * value * (1.0 - inner * inner) * scale * (
        1.0 + 3.0 * cubic * value * value
    )


def pick_kernel(slots_from, tokens_from, own, other, slots, tokens, done):
    dp, node = lax.axis_index("dp"), lax.axis_index("node")
    depth = slots.shape[0]
    experts = slots.shape[1] // 2
    step = 512
    lists = pltpu.make_async_copy(slots_from, slots, done.at[0])
    lists.start()
    copies = []
    for number, start in enumerate(range(0, tokens.shape[1], step)):
        cols = pl.ds(start, step)
        copies.append(
            pltpu.make_async_copy(tokens_from.at[:, cols], tokens.at[:, cols], done.at[number + 1])
        )
        copies[-1].start()
    lists.wait()
    lane = lax.broadcasted_iota(jnp.int32, slots.shape, 1)
    listed = slots[...]
    token = lax.broadcasted_iota(jnp.int32, (2 * depth, tokens.shape[0]), 1)
    columns = [
        jnp.sum(jnp.where(lane == target * experts + node // 2, listed, 0), axis=1, keepdims=True)
        for target in (dp, 1 - dp)
    ]
    onehot = jnp.where(token == jnp.concatenate(columns, axis=0), 1.0, 0.0).astype(BF16)
    for number, start in enumerate(range(0, tokens.shape[1], step)):
        cols = slice(start, start + step)
        copies[number].wait()
        rows = jnp.dot(onehot, tokens[:, cols], preferred_element_type=F32).astype(BF16)
        own[:, cols] = rows[:depth]
        other[:, cols] = rows[depth:]


def prepare_kernel(slots, grad, held, sent, onehot):
    dp, chip = lax.axis_index("dp"), lax.axis_index("chip")
    total = grad.shape[1]
    for blocks, out in ((HELD, held), (SENT, sent)):
        count = 32 * len(blocks)
        row = lax.broadcasted_iota(jnp.int32, (8, count), 1)
        block = row // 32
        half = row // 16 - 2 * block
        column = row - 16 * (row // 16) + 16 * jnp.where(half == 0, dp, 1 - dp)
        for number, offset in enumerate(blocks):
            first = lax.rem(chip + offset + 8, 8) * 32
            column = jnp.where(block == number, column + first, column)
        given = lax.broadcasted_iota(jnp.int32, (total, count), 0)
        order = jnp.where(given == column[:1], 1.0, 0.0).astype(BF16)
        out[...] = jnp.dot(grad[...], order, preferred_element_type=F32).astype(BF16)
    depth = slots.shape[0]
    experts = slots.shape[1] // 2
    tokens = onehot.shape[2]
    token = lax.broadcasted_iota(jnp.int32, (depth, tokens), 1)
    for half in range(2):
        listed = slots[:, half * experts : (half + 1) * experts]
        for expert in range(experts):
            column = listed[:, expert : expert + 1]
            onehot[half, expert * depth : (expert + 1) * depth, :] = jnp.where(
                token == column, 1.0, 0.0
            ).astype(BF16)


def fill(rows, *pieces):
    at = 0
    for ref in pieces:
        rows[at : at + ref.shape[0], :] = ref[...]
        at += ref.shape[0]


def expert_kernel(pieces, *refs):
    given, wt, grad = refs[:pieces], refs[pieces], refs[pieces + 1]
    parts, dh_out, rows = refs[pieces + 2 : -2], refs[-2], refs[-1]
    fill(rows, *given)
    pre = lax.dot_general(wt[...], rows[...], (((1,), (1,)), ((), ())), preferred_element_type=F32)
    dh = (grad[...].astype(F32) * gelu_slope(pre)).astype(BF16)
    dh_out[...] = dh
    step = 512
    for start in range(0, wt.shape[1], step):
        cols = slice(start, start + step)
        part = lax.dot_general(
            dh, wt[:, cols], (((0,), (0,)), ((), ())), preferred_element_type=F32
        ).astype(BF16)
        at = 0
        for out in parts:
            out[:, cols] = part[at : at + out.shape[0]]
            at += out.shape[0]


def join_kernel(x0, p2, m2, to_p, to_m):
    fill(to_p, x0, p2)
    fill(to_m, x0, m2)


def weight_kernel(dh_held, dh_sent, x0, p2, m2, p1, m1, far, out, rows, dh):
    fill(rows, x0, p2, m2, far, p1, m1)
    at = 0
    for ref in (dh_held, dh_sent):
        dh[:, at : at + ref.shape[1]] = ref[...]
        at += ref.shape[1]
    step = 512
    for start in range(0, out.shape[1], step):
        cols = slice(start, start + step)
        out[:, cols] = jnp.dot(dh[...], rows[:, cols], preferred_element_type=F32).astype(BF16)


def middle_kernel(keep, got_p, got_m, to_p, to_m):
    f = lambda value: value.astype(F32)
    to_m[...] = (f(keep[32:64]) + f(got_m[32:64])).astype(BF16)
    to_p[...] = (f(keep[64:96]) + f(got_p[32:64])).astype(BF16)


def across_kernel(keep, across, out):
    out[...] = keep[0:32].astype(F32) + across[...].astype(F32)


def last_kernel(near, got_p, got_m, from_p, from_m, own, other):
    for start, out in ((0, own), (16, other)):
        at = slice(start, start + 16)
        total = near[at]
        for ref in (got_p, got_m, from_p, from_m):
            total = total + ref[at].astype(F32)
        out[...] = total.astype(BF16)


def pack_kernel(own, other, out):
    dp = lax.axis_index("dp")
    nodes = out.shape[1]
    wide = own.shape[1] // nodes
    gap = jnp.zeros((own.shape[0], 128 - wide), BF16)
    low = jnp.where(dp == 0, own[...], other[...])
    high = jnp.where(dp == 0, other[...], own[...])
    for node in range(nodes):
        cols = slice(node * wide, (node + 1) * wide)
        out[0, node] = jnp.concatenate([low[:, cols], gap], axis=1)
        out[1, node] = jnp.concatenate([high[:, cols], gap], axis=1)


def spread_kernel(onehot, arrived, out):
    wide, tokens = out.shape
    total = jnp.zeros((128, tokens), F32)
    for half in range(2):
        for pair in range(2):
            got = arrived[half, :, pair].reshape(onehot.shape[1], 128)
            total += lax.dot_general(
                got, onehot[half], (((0,), (0,)), ((), ())), preferred_element_type=F32
            )
    out[...] = total[:wide]


def shape(rows, columns, dtype=BF16):
    return jax.ShapeDtypeStruct((rows, columns), dtype)


def body(tokens, slot_token, grad_act, w_up):
    tok_grp, width = tokens.shape
    hidden = w_up.shape[1]
    n_nodes = lax.axis_size("node")
    chips = lax.axis_size("chip")
    slots = slot_token[0, 0].T
    depth = slots.shape[0]
    wt = w_up.T
    grad = grad_act.T

    def shift(value, by):
        return lax.ppermute(value, "chip", [(c, (c + by) % chips) for c in range(chips)])

    def swap(value):
        return lax.ppermute(value, "dp", [(0, 1), (1, 0)])

    own, other = pl.pallas_call(
        pick_kernel,
        in_specs=[HBM] * 2,
        out_specs=[VMEM] * 2,
        out_shape=[shape(depth, width)] * 2,
        scratch_shapes=[
            pltpu.VMEM(slots.shape, jnp.int32),
            pltpu.VMEM(tokens.shape, BF16),
            pltpu.SemaphoreType.DMA((width // 512 + 1,)),
        ],
        compiler_params=pltpu.CompilerParams(vmem_limit_bytes=62 * 1024 * 1024),
    )(slots, tokens)
    x0 = jnp.concatenate([own, swap(other)], 0)

    def expert(rows, cotangent, sizes, cost=None):
        count = cotangent.shape[1]
        return pl.pallas_call(
            functools.partial(expert_kernel, len(rows)),
            in_specs=[VMEM] * (len(rows) + 2),
            out_specs=[VMEM] * (len(sizes) + 1),
            out_shape=[shape(size, width) for size in sizes] + [shape(hidden, count)],
            scratch_shapes=[pltpu.VMEM((count, width), BF16)],
            compiler_params=PARAMS,
            cost_estimate=cost
            or pl.CostEstimate(flops=4 * count * hidden * width, bytes_accessed=4000000, transcendentals=0),
        )(*rows, wt, cotangent)

    p2, m2 = shift(x0, 2), shift(x0, -2)
    far = shift(x0, 4)
    grad_held, grad_sent, onehot = pl.pallas_call(
        prepare_kernel,
        in_specs=[VMEM, VMEM],
        out_specs=[VMEM] * 3,
        out_shape=[
            shape(hidden, 128),
            shape(hidden, 128),
            jax.ShapeDtypeStruct((2, depth * n_nodes // 2, tok_grp), BF16),
        ],
        compiler_params=PARAMS,
    )(slots, grad)
    p2, grad_held, grad_sent, onehot = lax.optimization_barrier(
        (p2, grad_held, grad_sent, onehot)
    )
    to_p, to_m = pl.pallas_call(
        join_kernel,
        in_specs=[VMEM] * 3,
        out_specs=[VMEM] * 2,
        out_shape=[shape(64, width)] * 2,
        compiler_params=PARAMS,
        cost_estimate=WAIT,
    )(x0, p2, m2)
    p1, m1 = shift(to_p, 1), shift(to_m, -1)
    keep, to_far, dh_held = expert((x0, p2, m2, far), grad_held, (96, 32), WAIT)
    across = shift(to_far, 4)
    p1, keep, dh_held = lax.optimization_barrier((p1, keep, dh_held))
    to_m, to_p, dh_sent = expert((p1, m1), grad_sent, (64, 64))
    got_p, got_m = shift(to_p, 1), shift(to_m, -1)
    grad_wt = pl.pallas_call(
        weight_kernel,
        in_specs=[VMEM] * 8,
        out_specs=VMEM,
        out_shape=shape(hidden, width),
        scratch_shapes=[pltpu.VMEM((256, width), BF16), pltpu.VMEM((hidden, 256), BF16)],
        compiler_params=PARAMS,
        cost_estimate=pl.CostEstimate(flops=2 * 256 * hidden * width, bytes_accessed=5000000, transcendentals=0),
    )(dh_held, dh_sent, x0, p2, m2, p1, m1, far)
    near = pl.pallas_call(
        across_kernel,
        in_specs=[VMEM] * 2,
        out_specs=VMEM,
        out_shape=shape(32, width, F32),
        compiler_params=PARAMS,
        cost_estimate=WAIT,
    )(keep, across)
    got_p, got_m, near = lax.optimization_barrier((got_p, got_m, near))
    back_p, back_m = pl.pallas_call(
        middle_kernel,
        in_specs=[VMEM] * 3,
        out_specs=[VMEM] * 2,
        out_shape=[shape(32, width)] * 2,
        compiler_params=PARAMS,
        cost_estimate=WAIT,
    )(keep, got_p, got_m)
    from_p, from_m = shift(back_p, 2), shift(back_m, -2)
    from_p, from_m, grad_wt = lax.optimization_barrier((from_p, from_m, grad_wt))
    own_sum, other_sum = pl.pallas_call(
        last_kernel,
        in_specs=[VMEM] * 5,
        out_specs=[VMEM] * 2,
        out_shape=[shape(depth, width)] * 2,
        compiler_params=PARAMS,
    )(near, got_p, got_m, from_p, from_m)
    packed = pl.pallas_call(
        pack_kernel,
        in_specs=[VMEM] * 2,
        out_specs=VMEM,
        out_shape=jax.ShapeDtypeStruct((2, n_nodes, depth, 128), BF16),
        compiler_params=PARAMS,
    )(own_sum, other_sum)
    arrived = lax.all_to_all(
        packed.reshape(2 * n_nodes, depth, 128), ("dp", "node"), 0, 0, tiled=True
    )
    grad_xt = pl.pallas_call(
        spread_kernel,
        in_specs=[VMEM, VMEM],
        out_specs=VMEM,
        out_shape=shape(width // n_nodes, tok_grp, F32),
        compiler_params=PARAMS,
    )(onehot, arrived.reshape(2, n_nodes // 2, 2, depth, 128))
    return (grad_wt.T, grad_xt.T)


def solution(mesh):
    placed = (
        P(("dp", "chip"), None),
        P("dp", "chip", None, None),
        P(None, ("dp", "node", "chip")),
        P(None, ("dp", "node", "chip")),
    )
    return jax.shard_map(
        body,
        mesh=mesh,
        in_specs=placed,
        out_specs=(P(None, ("dp", "node", "chip")), P(("dp", "chip"), "node")),
        check_vma=False,
    )
```
